128 devices in a mesh: rep: 16 (over y, x), exp: 8 (over z, core).
Axes of the slice: x: 4, y: 4, z: 4, core: 2. Of those that a mesh axis runs over, the one named last changes fastest.
Arguments:
- grad_parts: float32 [16, 128, 1024, 384], P('rep', 'exp'), may hold values from -6 to 6
- momentum: bfloat16 [128, 1024, 384], P('exp', 'rep'), may hold values from -24 to 24
Outputs:
- update: bfloat16 [128, 1024, 384], P('exp', 'rep')
The draws below stay inside these ranges and needn't reach their ends.
All inputs are finite; a program needn't handle non-finite values.
Results may differ from the reference program's by a relative error of at most 0.0013.
Values may be sent and summed in bfloat16 or wider, within the bound.
No kernel may reach another device: no remote copies, remote signals or barrier semaphores. Data moves between devices by JAX's collectives and lax.ppermute only.
A program may use at most 128 MiB of HBM per device.

```python
import jax
import jax.numpy as jnp
from jax import lax

D = 1024
FF = 384
NS_ITERS = 5
EXPERTS = 128
N_REP = 16


def strengthened(drawn, rng, source, target, shards_of, factor):
    owner, partner = [(jnp.arange(drawn.shape[dim]) // (drawn.shape[dim] // shards_of)).reshape([-1 if axis == dim else 1 for axis in range(drawn.ndim)]) for dim in (source, target)]
    chosen = jax.random.permutation(rng, shards_of)[partner]
    strong = (owner == chosen) | (owner == (partner + shards_of // 2) % shards_of)
    return jnp.where(strong, factor * drawn, drawn)


def level_of(rng, shape, split, least, top_value):
    def one(position, parts):
        steps = jax.random.uniform(jax.random.fold_in(jax.random.fold_in(rng, 6), position), (parts,), jnp.float32, least / len(split), top_value / len(split))
        return jnp.repeat(jnp.exp(steps), shape[position] // parts).reshape((-1,) + (1,) * (len(shape) - position - 1))

    level = one(*split[0])
    for cut in split[1:]:
        level = level * one(*cut)
    return level


def noise(key, dims, spread, most, shards=(), kind=jnp.bfloat16):
    level = level_of(key, dims, shards, -0.22, 0.18) if shards else 1.0
    result = jax.random.normal(key, dims, jnp.float32) * spread * level
    return jnp.minimum(jnp.maximum(result, -most), most).astype(kind)


def noise_with(key, extent, spread, most, shards, heavy, kind=jnp.bfloat16):
    array = spread * jax.random.normal(key, extent, jnp.float32)
    if shards:
        array = array * level_of(key, extent, shards, -0.22, 0.18)
    return jnp.clip(strengthened(array, jax.random.fold_in(key, 3), *heavy), -most, most).astype(kind)


def setup_inputs(seed: int = 0) -> dict:
    key_of = jax.random.split(jax.random.key(seed), 3)
    return {
        "grad_parts": noise_with(key_of[0], (N_REP, EXPERTS, D, FF), 1.0, 6.0, ((0, 16), (1, 8)), (0, 2, 16, 2.0), jnp.float32),
        "momentum": noise(key_of[1], (EXPERTS, D, FF), 4.0, 24.0, ((0, 8), (1, 16))),
    }


def orthogonalize(step):
    high = lax.Precision.HIGHEST
    norm = jnp.sqrt(jnp.sum(step * step))
    x = step / (norm + 1e-07)
    for turn in range(NS_ITERS):
        a = jnp.dot(x.T, x, precision=high)
        b = -4.775 * a + 2.0315 * jnp.dot(a, a, precision=high)
        x = 3.4445 * x + jnp.dot(x, b, precision=high)
    return x

def reference(grad_parts, momentum):
    scale = float(max(D, FF)) ** 0.5

    def one_expert(index):
        grad = lax.optimization_barrier(jnp.sum(grad_parts[:, index], axis=0))
        new_momentum = 0.95 * momentum[index].astype(jnp.float32) + grad
        direction = grad + 0.95 * new_momentum
        return (scale * orthogonalize(direction)).astype(jnp.bfloat16)
    return lax.map(one_expert, jnp.arange(EXPERTS, dtype=jnp.int32))
```

```python
import functools

import jax
import jax.numpy as jnp
import numpy as np
from jax import lax
from jax.experimental import pallas as pl
from jax.experimental.pallas import tpu as pltpu
from jax.sharding import PartitionSpec as P

D = 1024
FF = 384
NS_ITERS = 5
QUARTER = D // 4
STRIP = 32
BAND = 64
GAIN = 1.0 + 0.95
BLEND = 0.95 * 0.95 / GAIN

ORDERS = ((0, 2, 1, 3), (2, 1, 3, 0), (1, 3, 0, 2), (3, 0, 2, 1))
SHIFTS = (11, 11, 10, 9)


def bits_of(rep):
    y, x = divmod(rep, 4)
    return (int(x in (1, 2)), int(x >= 2), int(y in (1, 2)), int(y >= 2))


def rep_of(bits):
    x = 2 * bits[1] + (bits[0] ^ bits[1])
    y = 2 * bits[3] + (bits[2] ^ bits[3])
    return 4 * y + x


def partners(bit):
    pairs = []
    for rep in range(16):
        bits = list(bits_of(rep))
        bits[bit] ^= 1
        pairs.append((rep, rep_of(bits)))
    return pairs


def expert_table():
    table = np.zeros((16, 4, 16), np.int32)
    for rep in range(16):
        for quarter, order in enumerate(ORDERS):
            for relative in range(16):
                bits = list(bits_of(rep))
                for place, bit in enumerate(order):
                    bits[bit] ^= (relative >> (3 - place)) & 1
                table[rep, quarter, relative] = rep_of(bits)
    return table


def encode(value, shift):
    scaled = value * float(2**shift)
    second = scaled * scaled
    fourth = second * second
    eighth = fourth * fourth
    return jnp.where(value < 0, -eighth, eighth).astype(jnp.bfloat16)


def decode(code, shift):
    code = code.astype(jnp.float32)
    size = jnp.maximum(jnp.abs(code), float(2.0**-126))
    return code * jnp.exp2(jnp.log2(size) * -0.875 - float(shift))


def step_kernel(quarter, step, info, parts_ref, momentum_ref, *refs):
    received, out_ref = refs[:-1], refs[-1]

    def total(rows):
        value = parts_ref[0, rows]
        for turn, ref in enumerate(received):
            value = value + decode(ref[0, rows], SHIFTS[turn])
        return value

    def strip(index, carry):
        rows = pl.ds(pl.multiple_of(index * STRIP, STRIP), STRIP)
        out_ref[0, rows] = encode(total(rows), SHIFTS[step])
        return carry

    lax.fori_loop(0, QUARTER // STRIP, strip, 0)

    @pl.when(info[16] == quarter)
    def _():
        def band(index, carry):
            start = pl.multiple_of(info[17] + index * STRIP, STRIP)
            rows = pl.ds(start, STRIP)
            held = momentum_ref[0, pl.ds(pl.multiple_of(index * STRIP, STRIP), STRIP)].astype(jnp.float32)
            out_ref[0, rows] = encode(total(rows) + BLEND * held, SHIFTS[step])
            return carry

        lax.fori_loop(0, BAND // STRIP, band, 0)


def step_call(quarter, step, info, parts, momentum, received):
    count = 8 >> step
    base = count

    def expert(index, info):
        return info[base + index]

    in_specs = [
        pl.BlockSpec((1, QUARTER, FF), lambda i, info: (expert(i, info), quarter, 0)),
        pl.BlockSpec((1, BAND, FF), lambda i, info: (expert(i, info), 0, 0)),
    ] + [pl.BlockSpec((1, QUARTER, FF), lambda i, info: (base + i, 0, 0)) for _ in received]
    size = count * QUARTER * FF
    return pl.pallas_call(
        functools.partial(step_kernel, quarter, step),
        grid_spec=pltpu.PrefetchScalarGridSpec(
            num_scalar_prefetch=1,
            grid=(count,),
            in_specs=in_specs,
            out_specs=pl.BlockSpec((1, QUARTER, FF), lambda i, info: (i, 0, 0)),
        ),
        out_shape=jax.ShapeDtypeStruct((count, QUARTER, FF), jnp.bfloat16),
        cost_estimate=pl.CostEstimate(
            flops=size * 16, bytes_accessed=size * (6 + 2 * step), transcendentals=2 * size * step
        ),
        name=f"codes_q{quarter}_s{step}",
    )(info, parts, momentum, *received)


def halves(value):
    high = value.astype(jnp.bfloat16)
    return high, (value - high.astype(jnp.float32)).astype(jnp.bfloat16)


def dot(left, right):
    return jnp.dot(left, right, preferred_element_type=jnp.float32)


def product(left, right):
    return dot(left[0], right[0]) + (dot(left[0], right[1]) + dot(left[1], right[0]))


def iterate_kernel(info, parts_ref, momentum_ref, *refs):
    received, out_ref, high_ref, low_ref, sum_ref = refs[:16], refs[16], refs[17], refs[18], refs[19]

    for quarter in range(4):
        mine = received[4 * quarter : 4 * quarter + 4]

        def strip(index, carry, quarter=quarter, mine=mine):
            inner = pl.ds(pl.multiple_of(index * STRIP, STRIP), STRIP)
            outer = pl.ds(pl.multiple_of(quarter * QUARTER + index * STRIP, STRIP), STRIP)
            value = parts_ref[0, outer]
            for turn, ref in enumerate(mine):
                value = value + decode(ref[0, inner], SHIFTS[turn])
            sum_ref[outer] = value
            return carry

        lax.fori_loop(0, QUARTER // STRIP, strip, 0)

    start = pl.multiple_of(info[16] * QUARTER + info[17], BAND)
    sum_ref[pl.ds(start, BAND)] += BLEND * momentum_ref[0].astype(jnp.float32)

    gram = jnp.zeros((FF, FF), jnp.float32)
    cross = jnp.zeros((FF, FF), jnp.float32)
    rows_in = (((0,), (0,)), ((), ()))
    for quarter in range(4):
        rows = pl.ds(quarter * QUARTER, QUARTER)
        high, low = halves(sum_ref[rows])
        high_ref[rows] = high
        low_ref[rows] = low
        gram += lax.dot_general(high, high, rows_in, preferred_element_type=jnp.float32)
        cross += lax.dot_general(high, low, rows_in, preferred_element_type=jnp.float32)
    gram += cross + cross.T

    row = lax.broadcasted_iota(jnp.int32, (FF, FF), 0)
    column = lax.broadcasted_iota(jnp.int32, (FF, FF), 1)
    on_diagonal = row == column
    squares = jnp.sum(jnp.where(on_diagonal, gram, 0.0))
    scale = 1.0 / (jnp.sqrt(jnp.full((1, 1), squares)) + 1e-07 / GAIN)
    a = gram * scale * scale
    power = None
    for turn in range(NS_ITERS):
        a_split = halves(a)
        b = -4.775 * a + 2.0315 * product(a_split, a_split)
        b_split = halves(b)
        if power is None:
            power = jnp.where(on_diagonal, 3.4445, 0.0) + b
        else:
            power = 3.4445 * power + product(halves(power), b_split)
        if turn < NS_ITERS - 1:
            once = 3.4445 * a + product(a_split, b_split)
            a = 3.4445 * once + product(halves(once), b_split)
    power_split = halves(power * (scale * float(max(D, FF)) ** 0.5))
    for quarter in range(4):
        rows = pl.ds(quarter * QUARTER, QUARTER)
        out_ref[rows] = product((high_ref[rows], low_ref[rows]), power_split).astype(jnp.bfloat16)


def iterate_call(info, parts, momentum, received):
    def own(i, info):
        return (info[0], 0, 0)

    in_specs = [
        pl.BlockSpec((1, D, FF), own),
        pl.BlockSpec((1, BAND, FF), own),
    ] + [pl.BlockSpec((1, QUARTER, FF), lambda i, info: (0, 0, 0)) for _ in received]
    return pl.pallas_call(
        iterate_kernel,
        grid_spec=pltpu.PrefetchScalarGridSpec(
            num_scalar_prefetch=1,
            grid=(1,),
            in_specs=in_specs,
            out_specs=pl.BlockSpec((D, FF), lambda i, info: (0, 0)),
            scratch_shapes=[
                pltpu.VMEM((D, FF), jnp.bfloat16),
                pltpu.VMEM((D, FF), jnp.bfloat16),
                pltpu.VMEM((D, FF), jnp.float32),
            ],
        ),
        out_shape=jax.ShapeDtypeStruct((D, FF), jnp.bfloat16),
        compiler_params=pltpu.CompilerParams(vmem_limit_bytes=40 * 1024 * 1024),
        cost_estimate=pl.CostEstimate(
            flops=3 * 2 * FF * FF * (17 * FF + 2 * D), bytes_accessed=6 * 1024 * 1024, transcendentals=0
        ),
        name="newton_schulz",
    )(info, parts, momentum, *received)


def local(grad_parts, momentum):
    parts = grad_parts[0]
    rep = lax.axis_index("rep")
    table = jnp.asarray(expert_table())[rep]
    place = jnp.stack([rep // 4, (rep % 4) * BAND]).astype(jnp.int32)
    infos = [jnp.concatenate([table[quarter], place]) for quarter in range(4)]
    received = [[] for _ in range(4)]
    for step in range(4):
        for quarter in range(4):
            codes = step_call(quarter, step, infos[quarter], parts, momentum, received[quarter])
            received[quarter].append(lax.ppermute(codes, "rep", partners(ORDERS[quarter][step])))
    update = iterate_call(infos[0], parts, momentum, sum(received, []))
    return lax.all_to_all(update.reshape(16, BAND, FF), "rep", split_axis=0, concat_axis=0, tiled=True)


def solution(mesh):
    return jax.shard_map(
        local,
        mesh=mesh,
        in_specs=(P("rep", "exp", None, None), P("exp", "rep", None)),
        out_specs=P("exp", "rep", None),
        check_vma=False,
    )
```

```python
import functools
import math

import jax
import jax.numpy as jnp
import numpy as np
from jax import lax
from jax.experimental import pallas as pl
from jax.experimental.pallas import tpu as pltpu
from jax.sharding import PartitionSpec as P

D = 1024
FF = 384
NS_ITERS = 5
QUARTER = D // 4
STRIP = 64
BAND = 64
GAIN = 1.0 + 0.95
BLEND = 0.95 * 0.95 / GAIN

ORDERS = ((3, 0, 2, 1), (1, 3, 0, 2), (2, 1, 3, 0), (0, 2, 1, 3))
SHIFTS = (11, 11, 10, 9)


def bits_of(rep):
    y, x = divmod(rep, 4)
    return (int(x in (1, 2)), int(x >= 2), int(y in (1, 2)), int(y >= 2))


def rep_of(bits):
    x = 2 * bits[1] + (bits[0] ^ bits[1])
    y = 2 * bits[3] + (bits[2] ^ bits[3])
    return 4 * y + x


def partners(bit):
    pairs = []
    for rep in range(16):
        bits = list(bits_of(rep))
        bits[bit] ^= 1
        pairs.append((rep, rep_of(bits)))
    return pairs


def expert_table():
    table = np.zeros((16, 128), np.int32)
    for rep in range(16):
        for quarter, order in enumerate(ORDERS):
            for relative in range(16):
                bits = list(bits_of(rep))
                for place, bit in enumerate(order):
                    bits[bit] ^= (relative >> (3 - place)) & 1
                table[rep, 16 * quarter + relative] = rep_of(bits)
        table[rep, 64:66] = rep // 4, rep % 4 * BAND
    return table


def encode(value, shift):
    scaled = value * float(2**shift)
    second = scaled * scaled
    fourth = second * second
    eighth = fourth * fourth
    return jnp.where(value < 0, -eighth, eighth).astype(jnp.bfloat16)


def decode(code, shift):
    code = code.astype(jnp.float32)
    size = jnp.maximum(jnp.abs(code), float(2.0**-126))
    return code * jnp.exp2(jnp.log(size) * (-0.875 / math.log(2.0)) - float(shift))


def fetches(quarter, entries, info, parts_ref, momentum_ref, held_ref, band_ref, sems, band_sems):
    rows = pl.ds(quarter * QUARTER, QUARTER)

    def raw(index):
        expert = info[16 * quarter + entries + index]
        return pltpu.make_async_copy(parts_ref.at[expert, rows], held_ref.at[index], sems.at[index])

    def band(index):
        expert = info[16 * quarter + entries + index]
        return pltpu.make_async_copy(momentum_ref.at[expert], band_ref.at[index], band_sems.at[index])

    def start():
        for index in range(8):
            raw(index).start()

        @pl.when(info[64] == quarter)
        def _():
            for index in range(8):
                band(index).start()

    def finish(index):
        raw(index).wait()

        @pl.when(info[64] == quarter)
        def _():
            band(index).wait()
            rows = pl.ds(pl.multiple_of(info[65], BAND), BAND)
            held_ref[index, rows] += BLEND * band_ref[index].astype(jnp.float32)

    return start, finish


FETCH_SCRATCH = (
    pltpu.VMEM((8, BAND, FF), jnp.bfloat16),
    pltpu.SemaphoreType.DMA((8,)),
    pltpu.SemaphoreType.DMA((8,)),
)


def encode_expert(held_ref, out_ref, index):
    for start in range(0, QUARTER, STRIP):
        rows = pl.ds(start, STRIP)
        out_ref[index, rows] = encode(held_ref[index, rows], SHIFTS[0])


def first_kernel(info, parts_ref, momentum_ref, out_ref, next_ref, held_ref, *scratch):
    start_now, finish_now = fetches(3, 8, info, parts_ref, momentum_ref, held_ref, *scratch[:3])
    start_next, finish_next = fetches(2, 8, info, parts_ref, momentum_ref, next_ref, *scratch[3:])
    start_now()
    start_next()

    def expert(index, carry):
        finish_now(index)
        encode_expert(held_ref, out_ref, index)
        return carry

    lax.fori_loop(0, 8, expert, 0)
    lax.fori_loop(0, 8, lambda index, carry: (finish_next(index), carry)[1], 0)


def later_kernel(quarter, info, parts_ref, momentum_ref, held_ref, out_ref, *rest):
    last = quarter == 0
    if not last:
        start_next, finish_next = fetches(quarter - 1, 8, info, parts_ref, momentum_ref, *rest)
        start_next()

    def expert(index, carry):
        encode_expert(held_ref, out_ref, index)
        return carry

    lax.fori_loop(0, 8, expert, 0)
    if not last:
        lax.fori_loop(0, 8, lambda index, carry: (finish_next(index), carry)[1], 0)


def first_calls(info, parts, momentum):
    size = 8 * QUARTER * FF
    whole = pl.BlockSpec(memory_space=pltpu.VMEM)
    raw = jax.ShapeDtypeStruct((8, QUARTER, FF), jnp.float32)
    codes = [None] * 4
    held = None
    for quarter in (3, 2, 1, 0):
        last = quarter == 0
        results = pl.pallas_call(
            first_kernel if held is None else functools.partial(later_kernel, quarter),
            in_specs=[
                pl.BlockSpec(memory_space=pltpu.SMEM),
                pl.BlockSpec(memory_space=pltpu.HBM),
                pl.BlockSpec(memory_space=pltpu.HBM),
            ]
            + [whole] * (held is not None),
            out_specs=[whole] * (1 if last else 2),
            scratch_shapes=[pltpu.VMEM((8, QUARTER, FF), jnp.float32)] * (held is None)
            + [*FETCH_SCRATCH] * ((held is None) + (not last)),
            out_shape=[jax.ShapeDtypeStruct((8, QUARTER, FF), jnp.bfloat16)] + [raw] * (not last),
            compiler_params=pltpu.CompilerParams(vmem_limit_bytes=40 * 1024 * 1024),
            cost_estimate=pl.CostEstimate(flops=size * 10, bytes_accessed=size * 6, transcendentals=0),
            name=f"first_q{quarter}",
        )(info, parts, momentum, *([] if held is None else [held]))
        codes[quarter] = results[0]
        held = results[-1]
    return codes


def keep_kernel(info, parts_ref, momentum_ref, *refs):
    held_refs, band_refs, sems, band_sems = refs[4:8], *refs[8:]
    pending = []
    for quarter, held_ref in enumerate(held_refs):
        start, finish = fetches(
            quarter, 0, info, parts_ref, momentum_ref, held_ref, band_refs, sems.at[quarter], band_sems
        )
        start()
        pending.append(finish)
    for finish in pending:
        lax.fori_loop(0, 8, lambda index, carry: (finish(index), carry)[1], 0)


def keep_call(info, parts, momentum, codes):
    size = 8 * QUARTER * FF
    whole = pl.BlockSpec(memory_space=pltpu.VMEM)
    return pl.pallas_call(
        keep_kernel,
        in_specs=[
            pl.BlockSpec(memory_space=pltpu.SMEM),
            pl.BlockSpec(memory_space=pltpu.HBM),
            pl.BlockSpec(memory_space=pltpu.HBM),
        ]
        + [pl.BlockSpec(memory_space=pl.ANY)] * 4,
        out_specs=[whole] * 4,
        scratch_shapes=[
            pltpu.VMEM((8, BAND, FF), jnp.bfloat16),
            pltpu.SemaphoreType.DMA((4, 8)),
            pltpu.SemaphoreType.DMA((8,)),
        ],
        out_shape=[jax.ShapeDtypeStruct((8, QUARTER, FF), jnp.float32)] * 4,
        compiler_params=pltpu.CompilerParams(vmem_limit_bytes=32 * 1024 * 1024),
        cost_estimate=pl.CostEstimate(flops=size, bytes_accessed=size * 16, transcendentals=0),
        name="keep",
    )(info, parts, momentum, *codes)


def step_kernel(step, kept_ref, *refs):
    received, out_ref = refs[:step], refs[step]
    count = out_ref.shape[0]

    def expert(index, carry):
        for start in range(0, QUARTER, STRIP):
            rows = pl.ds(start, STRIP)
            value = kept_ref[count + index, rows]
            for turn, ref in enumerate(received):
                value = value + decode(ref[count + index, rows], SHIFTS[turn])
            out_ref[index, rows] = encode(value, SHIFTS[step])
        return carry

    lax.fori_loop(0, count, expert, 0)


def step_call(quarter, step, kept, received):
    count = 8 >> step
    size = count * QUARTER * FF
    whole = pl.BlockSpec(memory_space=pltpu.VMEM)
    return pl.pallas_call(
        functools.partial(step_kernel, step),
        in_specs=[whole] * (1 + step),
        out_specs=whole,
        out_shape=jax.ShapeDtypeStruct((count, QUARTER, FF), jnp.bfloat16),
        compiler_params=pltpu.CompilerParams(vmem_limit_bytes=8 * 1024 * 1024),
        cost_estimate=pl.CostEstimate(
            flops=size * 16, bytes_accessed=size * (6 + 2 * step), transcendentals=2 * size * step
        ),
        name=f"codes_q{quarter}_s{step}",
    )(kept, *received)


def halves(value):
    high = value.astype(jnp.bfloat16)
    return high, (value - high.astype(jnp.float32)).astype(jnp.bfloat16)


def dot(left, right):
    return jnp.dot(left, right, preferred_element_type=jnp.float32)


def product(left, right):
    return dot(left[0], right[0]) + (dot(left[0], right[1]) + dot(left[1], right[0]))


def iterate_kernel(*refs):
    kept_refs, received, out_ref, high_ref, low_ref, sum_ref = refs[:4], refs[4:20], *refs[20:]
    for quarter, kept_ref in enumerate(kept_refs):
        mine = received[4 * quarter : 4 * quarter + 4]
        for start in range(0, QUARTER, STRIP):
            value = kept_ref[0, pl.ds(start, STRIP)]
            for turn, ref in enumerate(mine):
                value = value + decode(ref[0, pl.ds(start, STRIP)], SHIFTS[turn])
            sum_ref[pl.ds(quarter * QUARTER + start, STRIP)] = value

    gram = jnp.zeros((FF, FF), jnp.float32)
    cross = jnp.zeros((FF, FF), jnp.float32)
    rows_in = (((0,), (0,)), ((), ()))
    for quarter in range(4):
        rows = pl.ds(quarter * QUARTER, QUARTER)
        high, low = halves(sum_ref[rows])
        high_ref[rows] = high
        low_ref[rows] = low
        gram += lax.dot_general(high, high, rows_in, preferred_element_type=jnp.float32)
        cross += lax.dot_general(high, low, rows_in, preferred_element_type=jnp.float32)
    gram += cross + cross.T

    row = lax.broadcasted_iota(jnp.int32, (FF, FF), 0)
    column = lax.broadcasted_iota(jnp.int32, (FF, FF), 1)
    on_diagonal = row == column
    squares = jnp.sum(jnp.where(on_diagonal, gram, 0.0))
    scale = 1.0 / (jnp.sqrt(jnp.full((1, 1), squares)) + 1e-07 / GAIN)
    a = gram * scale * scale
    power = None
    for turn in range(NS_ITERS):
        a_split = halves(a)
        b = -4.775 * a + 2.0315 * product(a_split, a_split)
        b_split = halves(b)
        if power is None:
            power = jnp.where(on_diagonal, 3.4445, 0.0) + b
        else:
            power = 3.4445 * power + product(halves(power), b_split)
        if turn < NS_ITERS - 1:
            once = 3.4445 * a + product(a_split, b_split)
            a = 3.4445 * once + product(halves(once), b_split)
    power_split = halves(power * (scale * float(max(D, FF)) ** 0.5))
    for quarter in range(4):
        rows = pl.ds(quarter * QUARTER, QUARTER)
        out_ref[rows] = product((high_ref[rows], low_ref[rows]), power_split).astype(jnp.bfloat16)


def iterate_call(kept, received):
    whole = pl.BlockSpec(memory_space=pltpu.VMEM)
    return pl.pallas_call(
        iterate_kernel,
        in_specs=[whole] * (len(kept) + len(received)),
        out_specs=whole,
        scratch_shapes=[
            pltpu.VMEM((D, FF), jnp.bfloat16),
            pltpu.VMEM((D, FF), jnp.bfloat16),
            pltpu.VMEM((D, FF), jnp.float32),
        ],
        out_shape=jax.ShapeDtypeStruct((D, FF), jnp.bfloat16),
        compiler_params=pltpu.CompilerParams(vmem_limit_bytes=16 * 1024 * 1024),
        cost_estimate=pl.CostEstimate(
            flops=3 * 2 * FF * FF * (17 * FF + 2 * D), bytes_accessed=6 * 1024 * 1024, transcendentals=0
        ),
        name="newton_schulz",
    )(*kept, *received)


def local(grad_parts, momentum):
    parts = grad_parts[0]
    info = jnp.asarray(expert_table())[lax.axis_index("rep")]
    codes = first_calls(info, parts, momentum)
    kept = keep_call(info, parts, momentum, codes)
    received = [[] for _ in range(4)]
    for step in range(4):
        for quarter in range(4):
            if step:
                codes[quarter] = step_call(quarter, step, kept[quarter], received[quarter])
            received[quarter].append(
                lax.ppermute(codes[quarter], "rep", partners(ORDERS[quarter][step]))
            )
    update = iterate_call(kept, sum(received, []))
    return lax.all_to_all(update.reshape(16, BAND, FF), "rep", split_axis=0, concat_axis=0, tiled=True)


def solution(mesh):
    return jax.shard_map(
        local,
        mesh=mesh,
        in_specs=(P("rep", "exp", None, None), P("exp", "rep", None)),
        out_specs=P("exp", "rep", None),
        check_vma=False,
    )
```

```python
import functools
import math

import jax
import jax.numpy as jnp
from jax import lax
from jax.experimental import pallas as pl
from jax.experimental.pallas import tpu as pltpu
from jax.sharding import PartitionSpec as P

D = 1024
FF = 384
NS_ITERS = 5
QUARTER = D // 4
STRIP = 64
BAND = 64
SPLIT = 256
GAIN = 1.0 + 0.95
BLEND = 0.95 * 0.95 / GAIN

ORDERS = ((3, 0, 2, 1), (1, 3, 0, 2), (2, 1, 3, 0), (0, 2, 1, 3))
FLIPS = (1, 3, 4, 12)
SHIFTS = (3, 3, 2, 2)
BEND = 2


def partners(bit):
    return [(rep, rep ^ FLIPS[bit]) for rep in range(16)]


def expert_of(quarter, sent, index):
    first, *others = [FLIPS[bit] for bit in ORDERS[quarter]]
    expert = lax.axis_index("rep") ^ (first if sent else 0)
    for place, flip in enumerate(others):
        expert = expert ^ (((index >> (2 - place)) & 1) * flip)
    return expert


def encode(value, shift):
    scaled = value * float(2**shift)
    second = scaled * scaled
    fourth = second * second
    eighth = fourth * fourth
    size = eighth * jnp.maximum(eighth, float(2 ** (8 * BEND)))
    return jnp.where(value < 0, -size, size).astype(jnp.bfloat16)


def decode(code, shift):
    code = code.astype(jnp.float32)
    level = jnp.log(jnp.maximum(jnp.abs(code), float(2.0**-126)))
    steep = level * (-15 / 16 / math.log(2.0)) - float(shift)
    flat = level * (-7 / 8 / math.log(2.0)) - float(shift + BEND)
    return code * jnp.exp2(jnp.minimum(steep, flat))


def fetches(quarter, sent, parts_ref, momentum_ref, held_ref, band_ref, sems, band_sems):
    rows = pl.ds(quarter * QUARTER, QUARTER)
    rep = lax.axis_index("rep")
    has_band = (rep >> 2) == quarter

    def raw(index):
        expert = expert_of(quarter, sent, index)
        return pltpu.make_async_copy(parts_ref.at[expert, rows], held_ref.at[index], sems.at[index])

    def band(index):
        expert = expert_of(quarter, sent, index)
        return pltpu.make_async_copy(momentum_ref.at[expert], band_ref.at[index], band_sems.at[index])

    def start(index):
        @pl.when(has_band)
        def _():
            band(index).start()

        raw(index).start()

    def finish(index):
        raw(index).wait()

        @pl.when(has_band)
        def _():
            band(index).wait()
            rows = pl.ds(pl.multiple_of((rep & 3) * BAND, BAND), BAND)
            held_ref[index, rows] += BLEND * band_ref[index].astype(jnp.float32)

    return start, finish


FETCH_SCRATCH = (
    pltpu.VMEM((8, BAND, FF), jnp.bfloat16),
    pltpu.SemaphoreType.DMA((8,)),
    pltpu.SemaphoreType.DMA((8,)),
)


def encode_expert(held_ref, out_ref, index):
    for start in range(0, QUARTER, STRIP):
        rows = pl.ds(start, STRIP)
        out_ref[index, rows] = encode(held_ref[index, rows], SHIFTS[0])


def loop(body):
    def step(index, carry):
        body(index)
        return carry

    lax.fori_loop(0, 8, step, 0)


def first_kernel(parts_ref, momentum_ref, out_ref, next_ref, held_ref, *scratch):
    start_now, finish_now = fetches(3, True, parts_ref, momentum_ref, held_ref, *scratch[:3])
    start_next, finish_next = fetches(2, True, parts_ref, momentum_ref, next_ref, *scratch[3:])
    loop(start_now)

    def expert(index):
        finish_now(index)
        start_next(index)
        encode_expert(held_ref, out_ref, index)

    loop(expert)
    loop(finish_next)


def later_kernel(quarter, parts_ref, momentum_ref, held_ref, out_ref, *rest):
    last = quarter == 0
    if not last:
        start_next, finish_next = fetches(quarter - 1, True, parts_ref, momentum_ref, *rest)
        loop(start_next)
    loop(functools.partial(encode_expert, held_ref, out_ref))
    if not last:
        loop(finish_next)


def first_calls(parts, momentum):
    size = 8 * QUARTER * FF
    whole = pl.BlockSpec(memory_space=pltpu.VMEM)
    raw = jax.ShapeDtypeStruct((8, QUARTER, FF), jnp.float32)
    codes = [None] * 4
    held = None
    for quarter in (3, 2, 1, 0):
        last = quarter == 0
        results = pl.pallas_call(
            first_kernel if held is None else functools.partial(later_kernel, quarter),
            in_specs=[pl.BlockSpec(memory_space=pltpu.HBM)] * 2 + [whole] * (held is not None),
            out_specs=[whole] * (1 if last else 2),
            scratch_shapes=[pltpu.VMEM((8, QUARTER, FF), jnp.float32)] * (held is None)
            + [*FETCH_SCRATCH] * ((held is None) + (not last)),
            out_shape=[jax.ShapeDtypeStruct((8, QUARTER, FF), jnp.bfloat16)] + [raw] * (not last),
            compiler_params=pltpu.CompilerParams(vmem_limit_bytes=40 * 1024 * 1024),
            cost_estimate=pl.CostEstimate(flops=size * 10, bytes_accessed=size * 6, transcendentals=0),
            name=f"first_q{quarter}",
        )(parts, momentum, *([] if held is None else [held]))
        codes[quarter] = results[0]
        held = results[-1]
    return codes


def keep_kernel(parts_ref, momentum_ref, *refs):
    held_refs, band_refs, sems, band_sems = refs[4:8], *refs[8:]
    pending = []
    for quarter, held_ref in enumerate(held_refs):
        start, finish = fetches(
            quarter, False, parts_ref, momentum_ref, held_ref, band_refs, sems.at[quarter], band_sems
        )
        loop(start)
        pending.append(finish)
    for finish in pending:
        loop(finish)


def keep_call(parts, momentum, codes):
    size = 8 * QUARTER * FF
    whole = pl.BlockSpec(memory_space=pltpu.VMEM)
    return pl.pallas_call(
        keep_kernel,
        in_specs=[pl.BlockSpec(memory_space=pltpu.HBM)] * 2 + [pl.BlockSpec(memory_space=pl.ANY)] * 4,
        out_specs=[whole] * 4,
        scratch_shapes=[
            pltpu.VMEM((8, BAND, FF), jnp.bfloat16),
            pltpu.SemaphoreType.DMA((4, 8)),
            pltpu.SemaphoreType.DMA((8,)),
        ],
        out_shape=[jax.ShapeDtypeStruct((8, QUARTER, FF), jnp.float32)] * 4,
        compiler_params=pltpu.CompilerParams(vmem_limit_bytes=32 * 1024 * 1024),
        cost_estimate=pl.CostEstimate(flops=size, bytes_accessed=size * 16, transcendentals=0),
        name="keep",
    )(parts, momentum, *codes)


def step_kernel(step, kept_ref, *refs):
    received, out_ref = refs[:step], refs[step]
    count = out_ref.shape[0]

    def expert(index, carry):
        for start in range(0, QUARTER, STRIP):
            rows = pl.ds(start, STRIP)
            value = kept_ref[count + index, rows]
            for turn, ref in enumerate(received):
                value = value + decode(ref[count + index, rows], SHIFTS[turn])
            out_ref[index, rows] = encode(value, SHIFTS[step])
        return carry

    lax.fori_loop(0, count, expert, 0)


def step_call(quarter, step, kept, received):
    count = 8 >> step
    size = count * QUARTER * FF
    whole = pl.BlockSpec(memory_space=pltpu.VMEM)
    return pl.pallas_call(
        functools.partial(step_kernel, step),
        in_specs=[whole] * (1 + step),
        out_specs=whole,
        out_shape=jax.ShapeDtypeStruct((count, QUARTER, FF), jnp.bfloat16),
        compiler_params=pltpu.CompilerParams(vmem_limit_bytes=8 * 1024 * 1024),
        cost_estimate=pl.CostEstimate(
            flops=size * 16, bytes_accessed=size * (6 + 2 * step), transcendentals=2 * size * step
        ),
        name=f"codes_q{quarter}_s{step}",
    )(kept, *received)


def halves(value):
    high = value.astype(jnp.bfloat16)
    return high, (value - high.astype(jnp.float32)).astype(jnp.bfloat16)


def dot(left, right):
    return jnp.dot(left, right, preferred_element_type=jnp.float32)


def wide(left):
    return jnp.concatenate([left[0], left[1], left[0]], axis=1)


def tall(right):
    return jnp.concatenate([right[0], right[0], right[1]], axis=0)


def symmetric(left, right):
    left, right = wide(left), tall(right)
    most = dot(left, right[:, :SPLIT])
    corner = dot(left[SPLIT:], right[:, SPLIT:])
    return jnp.concatenate([most, jnp.concatenate([most[SPLIT:].T, corner], axis=0)], axis=1)


def gram_part(kept_refs, received, high_ref, low_ref):
    part = None
    for quarter, kept_ref in enumerate(kept_refs):
        mine = received[4 * quarter : 4 * quarter + 4]
        for start in range(0, QUARTER, STRIP):
            value = kept_ref[0, pl.ds(start, STRIP)]
            for turn, ref in enumerate(mine):
                value = value + decode(ref[0, pl.ds(start, STRIP)], SHIFTS[turn])
            rows = pl.ds(quarter * QUARTER + start, STRIP)
            high_ref[rows], low_ref[rows] = halves(value)
        rows = pl.ds(quarter * QUARTER, QUARTER)
        high = high_ref[rows]
        more = dot(high.T, jnp.concatenate([high, low_ref[rows]], axis=1))
        part = more if part is None else part + more
    return part


def gather_kernel(*refs):
    kept_refs, received, high_ref, low_ref, part_ref = refs[:3], refs[3:15], *refs[15:]
    part_ref[...] = gram_part(kept_refs, received, high_ref, low_ref)


def gather_call(kept, received):
    whole = pl.BlockSpec(memory_space=pltpu.VMEM)
    rows = QUARTER * len(kept)
    split = jax.ShapeDtypeStruct((rows, FF), jnp.bfloat16)
    return pl.pallas_call(
        gather_kernel,
        in_specs=[whole] * (len(kept) + len(received)),
        out_specs=[whole] * 3,
        out_shape=[split, split, jax.ShapeDtypeStruct((FF, 2 * FF), jnp.float32)],
        compiler_params=pltpu.CompilerParams(vmem_limit_bytes=16 * 1024 * 1024),
        cost_estimate=pl.CostEstimate(
            flops=4 * rows * FF * FF, bytes_accessed=16 * rows * FF, transcendentals=8 * rows * FF
        ),
        name="gather",
    )(*kept, *received)


def iterate_kernel(kept_ref, *refs):
    received, early_high, early_low, part_ref, out_ref, high_ref, low_ref = refs[:4], *refs[4:]
    part = part_ref[...] + gram_part([kept_ref], received, high_ref, low_ref)
    gram = part[:, :FF] + (part[:, FF:] + part[:, FF:].T)

    row = lax.broadcasted_iota(jnp.int32, (FF, FF), 0)
    column = lax.broadcasted_iota(jnp.int32, (FF, FF), 1)
    on_diagonal = row == column
    squares = jnp.sum(jnp.where(on_diagonal, gram, 0.0))
    scale = 1.0 / (jnp.sqrt(jnp.full((1, 1), squares)) + 1e-07 / GAIN)
    a = gram * scale * scale
    power = None
    for turn in range(NS_ITERS):
        a_split = halves(a)
        b = -4.775 * a + 2.0315 * symmetric(a_split, a_split)
        b_split = halves(b)
        if power is None:
            power = jnp.where(on_diagonal, 3.4445, 0.0) + b
        else:
            power = 3.4445 * power + symmetric(halves(power), b_split)
        if turn < NS_ITERS - 1:
            once = 3.4445 * a + symmetric(a_split, b_split)
            a = 3.4445 * once + symmetric(halves(once), b_split)
    power_split = tall(halves(power * (scale * float(max(D, FF)) ** 0.5)))
    for quarter in range(4):
        rows = pl.ds(quarter * QUARTER, QUARTER)
        if quarter:
            early = pl.ds((quarter - 1) * QUARTER, QUARTER)
            left = (early_high[early], early_low[early])
        else:
            left = (high_ref[...], low_ref[...])
        out_ref[rows] = dot(wide(left), power_split).astype(jnp.bfloat16)


def iterate_call(kept, received, early):
    whole = pl.BlockSpec(memory_space=pltpu.VMEM)
    return pl.pallas_call(
        iterate_kernel,
        in_specs=[whole] * (1 + len(received) + len(early)),
        out_specs=whole,
        scratch_shapes=[pltpu.VMEM((QUARTER, FF), jnp.bfloat16)] * 2,
        out_shape=jax.ShapeDtypeStruct((D, FF), jnp.bfloat16),
        compiler_params=pltpu.CompilerParams(vmem_limit_bytes=16 * 1024 * 1024),
        cost_estimate=pl.CostEstimate(
            flops=3 * 2 * FF * FF * (17 * FF + D), bytes_accessed=6 * 1024 * 1024, transcendentals=0
        ),
        name="newton_schulz",
    )(kept, *received, *early)


def local(grad_parts, momentum):
    parts = grad_parts[0]
    codes = first_calls(parts, momentum)
    kept = keep_call(parts, momentum, codes)
    received = [[] for _ in range(4)]
    for step in range(4):
        for quarter in range(4):
            if step:
                codes[quarter] = step_call(quarter, step, kept[quarter], received[quarter])
            received[quarter].append(
                lax.ppermute(codes[quarter], "rep", partners(ORDERS[quarter][step]))
            )
    early = gather_call(kept[1:], sum(received[1:], []))
    update = iterate_call(kept[0], received[0], early)
    return lax.all_to_all(update.reshape(16, BAND, FF), "rep", split_axis=0, concat_axis=0, tiled=True)


def solution(mesh):
    return jax.shard_map(
        local,
        mesh=mesh,
        in_specs=(P("rep", "exp", None, None), P("exp", "rep", None)),
        out_specs=P("exp", "rep", None),
        check_vma=False,
    )
```

```python
import functools
import math

import jax
import jax.numpy as jnp
from jax import lax
from jax.experimental import pallas as pl
from jax.experimental.pallas import tpu as pltpu
from jax.sharding import PartitionSpec as P

D = 1024
FF = 384
NS_ITERS = 5
ROWS = (240, 256, 256, 272)
FIRST = (784, 528, 272, 0)
PIECE = 16
STRIP = 64
BAND = 64
SPLIT = 256
BLOCK = 256
GAIN = 1.0 + 0.95
BLEND = 0.95 * 0.95 / GAIN

ORDERS = ((3, 0, 2, 1), (1, 3, 0, 2), (2, 1, 3, 0), (0, 2, 1, 3))
FLIPS = (1, 3, 4, 12)
SHIFT = 8
POWER = 9


def partners(bit):
    return [(rep, rep ^ FLIPS[bit]) for rep in range(16)]


def expert_of(quarter, sent, index):
    first, *others = [FLIPS[bit] for bit in ORDERS[quarter]]
    expert = lax.axis_index("rep") ^ (first if sent else 0)
    for place, flip in enumerate(others):
        expert = expert ^ (((index >> (2 - place)) & 1) * flip)
    return expert


def encode(value):
    second = value * value
    fourth = second * second
    return (fourth * fourth * value).astype(jnp.bfloat16)


def decode(code):
    code = code.astype(jnp.float32)
    level = jnp.log(jnp.maximum(jnp.abs(code), float(2.0**-126)))
    return code * jnp.exp2(level * ((1 / POWER - 1) / math.log(2.0)))


def raw_copy(quarter, sent, parts_ref, held_ref, sems, index):
    rows = pl.ds(FIRST[quarter], ROWS[quarter])
    expert = expert_of(quarter, sent, index)
    return pltpu.make_async_copy(parts_ref.at[expert, rows], held_ref.at[index], sems.at[index])


def on_band(quarter, body):
    low, count = FIRST[quarter], ROWS[quarter]
    band_low = lax.axis_index("rep") * BAND

    @pl.when((band_low < low + count) & (band_low + BAND > low))
    def _():
        for start in range(0, BAND, PIECE):
            row = band_low + start - low

            @pl.when((row >= 0) & (row < count))
            def _(start=start, row=row):
                body(pl.ds(pl.multiple_of(row, PIECE), PIECE), pl.ds(start, PIECE))


def strips(count):
    return [pl.ds(start, min(STRIP, count - start)) for start in range(0, count, STRIP)]


def loop(count, body):
    def step(index, carry):
        body(index)
        return carry

    lax.fori_loop(0, count, step, 0)


def fetch_kernel(parts_ref, held_ref, sems):
    loop(8, lambda index: raw_copy(3, True, parts_ref, held_ref, sems, index).start())
    loop(8, lambda index: raw_copy(3, True, parts_ref, held_ref, sems, index).wait())


def first_kernel(quarter, parts_ref, momentum_ref, held_ref, out_ref, *rest):
    if rest:
        loop(8, lambda index: raw_copy(quarter - 1, True, parts_ref, *rest, index).start())

    def expert(index):
        for rows in strips(ROWS[quarter]):
            out_ref[index, rows] = encode(held_ref[index, rows] * float(2**SHIFT))

        def blend(rows, band):
            held = momentum_ref[expert_of(quarter, True, index), band].astype(jnp.float32)
            out_ref[index, rows] = encode((held_ref[index, rows] + BLEND * held) * float(2**SHIFT))

        on_band(quarter, blend)

    loop(8, expert)
    if rest:
        loop(8, lambda index: raw_copy(quarter - 1, True, parts_ref, *rest, index).wait())


def first_calls(parts, momentum):
    hbm = pl.BlockSpec(memory_space=pltpu.HBM)
    whole = pl.BlockSpec(memory_space=pltpu.VMEM)
    params = pltpu.CompilerParams(vmem_limit_bytes=40 * 1024 * 1024)

    def raw(quarter):
        return jax.ShapeDtypeStruct((8, ROWS[quarter], FF), jnp.float32)

    held = pl.pallas_call(
        fetch_kernel,
        in_specs=[hbm],
        out_specs=whole,
        scratch_shapes=[pltpu.SemaphoreType.DMA((8,))],
        out_shape=raw(3),
        compiler_params=params,
        cost_estimate=pl.CostEstimate(flops=0, bytes_accessed=64 * ROWS[3] * FF, transcendentals=0),
        name="fetch",
    )(parts)
    codes = [None] * 4
    for quarter in (3, 2, 1, 0):
        more = quarter > 0
        size = 8 * ROWS[quarter] * FF
        results = pl.pallas_call(
            functools.partial(first_kernel, quarter),
            in_specs=[hbm, whole, whole],
            out_specs=[whole] * (1 + more),
            scratch_shapes=[pltpu.SemaphoreType.DMA((8,))] * more,
            out_shape=[jax.ShapeDtypeStruct((8, ROWS[quarter], FF), jnp.bfloat16)] + [raw(quarter - 1)] * more,
            compiler_params=params,
            cost_estimate=pl.CostEstimate(flops=size * 10, bytes_accessed=size * 6, transcendentals=0),
            name=f"first_q{quarter}",
        )(parts, momentum, held)
        codes[quarter] = results[0]
        held = results[-1]
    return codes


def keep_kernel(parts_ref, momentum_ref, *refs):
    held_refs, sems = refs[4:8], refs[8]

    def copy(quarter, index):
        return raw_copy(quarter, False, parts_ref, held_refs[quarter], sems.at[quarter], index)

    for quarter in range(4):
        loop(8, lambda index, quarter=quarter: copy(quarter, index).start())
    for quarter, held_ref in enumerate(held_refs):

        def expert(index, quarter=quarter, held_ref=held_ref):
            copy(quarter, index).wait()
            for rows in strips(ROWS[quarter]):
                held_ref[index, rows] = held_ref[index, rows] * float(2**SHIFT)

            def blend(rows, band):
                held = momentum_ref[expert_of(quarter, False, index), band].astype(jnp.float32)
                held_ref[index, rows] += BLEND * float(2**SHIFT) * held

            on_band(quarter, blend)

        loop(8, expert)


def keep_call(parts, momentum, codes):
    whole = pl.BlockSpec(memory_space=pltpu.VMEM)
    return pl.pallas_call(
        keep_kernel,
        in_specs=[pl.BlockSpec(memory_space=pltpu.HBM), whole] + [pl.BlockSpec(memory_space=pl.ANY)] * 4,
        out_specs=[whole] * 4,
        scratch_shapes=[pltpu.SemaphoreType.DMA((4, 8))],
        out_shape=[jax.ShapeDtypeStruct((8, rows, FF), jnp.float32) for rows in ROWS],
        compiler_params=pltpu.CompilerParams(vmem_limit_bytes=32 * 1024 * 1024),
        cost_estimate=pl.CostEstimate(flops=8 * D * FF, bytes_accessed=64 * D * FF, transcendentals=0),
        name="keep",
    )(parts, momentum, *codes)


def fold_kernel(*refs):
    kept_refs, received, out_refs = refs[:4], refs[4:8], refs[9:]
    for kept_ref, ref, out_ref in zip(kept_refs, received, out_refs):

        def expert(index, kept_ref=kept_ref, ref=ref, out_ref=out_ref):
            for rows in strips(out_ref.shape[1]):
                out_ref[index, rows] = kept_ref[index, rows] + decode(ref[index, rows])

        loop(4, expert)


def fold_call(kept, received, after):
    whole = pl.BlockSpec(memory_space=pltpu.VMEM)
    return pl.pallas_call(
        fold_kernel,
        in_specs=[whole] * 8 + [pl.BlockSpec(memory_space=pl.ANY)],
        out_specs=[whole] * 4,
        out_shape=[jax.ShapeDtypeStruct((4, rows, FF), jnp.float32) for rows in ROWS],
        compiler_params=pltpu.CompilerParams(vmem_limit_bytes=8 * 1024 * 1024),
        cost_estimate=pl.CostEstimate(flops=32 * D * FF, bytes_accessed=40 * D * FF, transcendentals=8 * D * FF),
        name="fold",
    )(*kept, *received, after)


def step_kernel(place, base_ref, *refs):
    received, out_ref = refs[:-1], refs[-1]

    def expert(index):
        for rows in strips(out_ref.shape[1]):
            value = base_ref[place + index, rows]
            for ref in received:
                value = value + decode(ref[place + index, rows])
            out_ref[index, rows] = encode(value)

    loop(out_ref.shape[0], expert)


def step_call(quarter, step, base, received):
    count = 8 >> step
    size = count * ROWS[quarter] * FF
    whole = pl.BlockSpec(memory_space=pltpu.VMEM)
    return pl.pallas_call(
        functools.partial(step_kernel, count),
        in_specs=[whole] * (1 + len(received)),
        out_specs=whole,
        out_shape=jax.ShapeDtypeStruct((count, ROWS[quarter], FF), jnp.bfloat16),
        compiler_params=pltpu.CompilerParams(vmem_limit_bytes=8 * 1024 * 1024),
        cost_estimate=pl.CostEstimate(
            flops=size * 16, bytes_accessed=size * (6 + 2 * step), transcendentals=2 * size * step
        ),
        name=f"codes_q{quarter}_s{step}",
    )(base, *received)


def halves(value):
    high = value.astype(jnp.bfloat16)
    return high, (value - high.astype(jnp.float32)).astype(jnp.bfloat16)


def dot(left, right):
    return jnp.dot(left, right, preferred_element_type=jnp.float32)


def wide(left):
    return jnp.concatenate([left[0], left[1], left[0]], axis=1)


def tall(right):
    return jnp.concatenate([right[0], right[0], right[1]], axis=0)


def symmetric(left, right):
    left, right = wide(left), tall(right)
    most = dot(left, right[:, :SPLIT])
    corner = dot(left[SPLIT:], right[:, SPLIT:])
    return jnp.concatenate([most, jnp.concatenate([most[SPLIT:].T, corner], axis=0)], axis=1)


def split_sums(kept_ref, received, high_ref, low_ref, first):
    for rows in strips(kept_ref.shape[1]):
        value = kept_ref[0, rows]
        for ref in received:
            value = value + decode(ref[0, rows])
        out = pl.ds(first + rows.start, rows.size)
        high_ref[out], low_ref[out] = halves(value)


def gram_part(high_ref, low_ref):
    part = None
    for start in range(0, high_ref.shape[0] - BLOCK + 1, BLOCK):
        rows = pl.ds(start, BLOCK)
        high = high_ref[rows]
        more = dot(high.T, jnp.concatenate([high, low_ref[rows]], axis=1))
        part = more if part is None else part + more
    return part


def gather_kernel(*refs):
    kept_refs, received, high_ref, low_ref, part_ref = refs[:3], refs[3:12], *refs[12:]
    for place, kept_ref in enumerate(kept_refs):
        split_sums(kept_ref, received[3 * place : 3 * place + 3], high_ref, low_ref, FIRST[1 + place])
    part_ref[...] = gram_part(high_ref, low_ref)


def gather_call(kept, received):
    whole = pl.BlockSpec(memory_space=pltpu.VMEM)
    rows = FIRST[0]
    split = jax.ShapeDtypeStruct((rows, FF), jnp.bfloat16)
    return pl.pallas_call(
        gather_kernel,
        in_specs=[whole] * (len(kept) + len(received)),
        out_specs=[whole] * 3,
        out_shape=[split, split, jax.ShapeDtypeStruct((FF, 2 * FF), jnp.float32)],
        compiler_params=pltpu.CompilerParams(vmem_limit_bytes=16 * 1024 * 1024),
        cost_estimate=pl.CostEstimate(
            flops=4 * rows * FF * FF, bytes_accessed=16 * rows * FF, transcendentals=8 * rows * FF
        ),
        name="gather",
    )(*kept, *received)


def iterate_kernel(kept_ref, *refs):
    received, early_high, early_low, part_ref, out_ref, high_ref, low_ref = refs[:3], *refs[3:]
    over = FIRST[0] % BLOCK
    high_ref[pl.ds(0, over)] = early_high[pl.ds(FIRST[0] - over, over)]
    low_ref[pl.ds(0, over)] = early_low[pl.ds(FIRST[0] - over, over)]
    split_sums(kept_ref, received, high_ref, low_ref, over)
    part = part_ref[...] + gram_part(high_ref, low_ref)
    gram = part[:, :FF] + (part[:, FF:] + part[:, FF:].T)

    row = lax.broadcasted_iota(jnp.int32, (FF, FF), 0)
    column = lax.broadcasted_iota(jnp.int32, (FF, FF), 1)
    on_diagonal = row == column
    squares = jnp.sum(jnp.where(on_diagonal, gram, 0.0))
    scale = 1.0 / (jnp.sqrt(jnp.full((1, 1), squares)) + 1e-07 / GAIN * 2**SHIFT)
    a = gram * scale * scale
    power = None
    for turn in range(NS_ITERS):
        a_split = halves(a)
        b = -4.775 * a + 2.0315 * symmetric(a_split, a_split)
        b_split = halves(b)
        if power is None:
            power = jnp.where(on_diagonal, 3.4445, 0.0) + b
        else:
            power = 3.4445 * power + symmetric(halves(power), b_split)
        if turn < NS_ITERS - 1:
            once = 3.4445 * a + symmetric(a_split, b_split)
            a = 3.4445 * once + symmetric(halves(once), b_split)
    power_split = tall(halves(power * (scale * float(max(D, FF)) ** 0.5)))
    for start in range(0, D, BLOCK):
        rows = pl.ds(start, BLOCK)
        if start + BLOCK <= FIRST[0]:
            left = (early_high[rows], early_low[rows])
        else:
            left = (high_ref[...], low_ref[...])
        out_ref[rows] = dot(wide(left), power_split).astype(jnp.bfloat16)


def iterate_call(kept, received, early):
    whole = pl.BlockSpec(memory_space=pltpu.VMEM)
    return pl.pallas_call(
        iterate_kernel,
        in_specs=[whole] * (1 + len(received) + len(early)),
        out_specs=whole,
        scratch_shapes=[pltpu.VMEM((BLOCK, FF), jnp.bfloat16)] * 2,
        out_shape=jax.ShapeDtypeStruct((D, FF), jnp.bfloat16),
        compiler_params=pltpu.CompilerParams(vmem_limit_bytes=16 * 1024 * 1024),
        cost_estimate=pl.CostEstimate(
            flops=3 * 2 * FF * FF * (17 * FF + D), bytes_accessed=6 * 1024 * 1024, transcendentals=0
        ),
        name="newton_schulz",
    )(kept, *received, *early)


def local(grad_parts, momentum):
    parts = grad_parts[0]

    def send(codes, step):
        return [lax.ppermute(codes[quarter], "rep", partners(ORDERS[quarter][step])) for quarter in range(4)]

    codes = first_calls(parts, momentum)
    kept = keep_call(parts, momentum, codes)
    first = send(codes, 0)
    codes = [step_call(quarter, 1, kept[quarter], [first[quarter]]) for quarter in range(4)]
    base = fold_call(kept, first, codes[0])
    second = send(codes, 1)
    codes = [step_call(quarter, 2, base[quarter], [second[quarter]]) for quarter in range(4)]
    third = send(codes, 2)
    codes = [step_call(quarter, 3, base[quarter], [second[quarter], third[quarter]]) for quarter in range(4)]
    received = list(zip(second, third, send(codes, 3)))
    early = gather_call(base[1:], sum(received[1:], ()))
    update = iterate_call(base[0], received[0], early)
    return lax.all_to_all(update.reshape(16, BAND, FF), "rep", split_axis=0, concat_axis=0, tiled=True)


def solution(mesh):
    return jax.shard_map(
        local,
        mesh=mesh,
        in_specs=(P("rep", "exp", None, None), P("exp", "rep", None)),
        out_specs=P("exp", "rep", None),
        check_vma=False,
    )
```

```python
import functools
import math

import jax
import jax.numpy as jnp
from jax import lax
from jax.experimental import pallas as pl
from jax.experimental.pallas import tpu as pltpu
from jax.sharding import PartitionSpec as P

D = 1024
FF = 384
NS_ITERS = 5
ROWS = (240, 256, 256, 272)
FIRST = (784, 528, 272, 0)
PIECE = 16
STRIP = 64
BAND = 64
SPLIT = 256
BLOCK = 256
GAIN = 1.0 + 0.95
BLEND = 0.95 * 0.95 / GAIN

ORDERS = ((3, 0, 2, 1), (1, 3, 0, 2), (2, 1, 3, 0), (0, 2, 1, 3))
FLIPS = (1, 3, 4, 12)
SHIFT = 8
POWER = 9


def flips_of(quarter, core):
    return [FLIPS[bit] for bit in ORDERS[(quarter + 3 * core) % 4]]


def partners(quarter, step):
    pairs = []
    for device in range(128):
        rep, group = divmod(device, 8)
        pairs.append((device, 8 * (rep ^ flips_of(quarter, group % 2)[step]) + group))
    return pairs


def expert_of(quarter, sent, index):
    core = lax.axis_index("exp") & 1
    first, *others = [zero + core * (one - zero) for zero, one in zip(flips_of(quarter, 0), flips_of(quarter, 1))]
    expert = lax.axis_index("rep")
    if sent:
        expert = expert ^ first
    for place, flip in enumerate(others):
        expert = expert ^ (((index >> (2 - place)) & 1) * flip)
    return expert


def encode(value):
    second = value * value
    fourth = second * second
    return (fourth * fourth * value).astype(jnp.bfloat16)


def decode(code):
    code = code.astype(jnp.float32)
    level = jnp.log(jnp.maximum(jnp.abs(code), float(2.0**-126)))
    return code * jnp.exp2(level * ((1 / POWER - 1) / math.log(2.0)))


def raw_copy(quarter, sent, parts_ref, held_ref, sems, index):
    rows = pl.ds(FIRST[quarter], ROWS[quarter])
    expert = expert_of(quarter, sent, index)
    return pltpu.make_async_copy(parts_ref.at[expert, rows], held_ref.at[index], sems.at[index])


def on_band(quarter, body):
    low, count = FIRST[quarter], ROWS[quarter]
    band_low = lax.axis_index("rep") * BAND

    @pl.when((band_low < low + count) & (band_low + BAND > low))
    def _():
        for start in range(0, BAND, PIECE):
            row = band_low + start - low

            @pl.when((row >= 0) & (row < count))
            def _(start=start, row=row):
                body(pl.ds(pl.multiple_of(row, PIECE), PIECE), pl.ds(start, PIECE))


def strips(count):
    return [pl.ds(start, min(STRIP, count - start)) for start in range(0, count, STRIP)]


def loop(count, body):
    def step(index, carry):
        body(index)
        return carry

    lax.fori_loop(0, count, step, 0)


def fetch_kernel(parts_ref, held_ref, sems):
    loop(8, lambda index: raw_copy(3, True, parts_ref, held_ref, sems, index).start())
    loop(8, lambda index: raw_copy(3, True, parts_ref, held_ref, sems, index).wait())


def first_kernel(quarter, parts_ref, momentum_ref, held_ref, out_ref, *rest):
    if rest:
        loop(8, lambda index: raw_copy(quarter - 1, True, parts_ref, *rest, index).start())

    def expert(index):
        for rows in strips(ROWS[quarter]):
            out_ref[index, rows] = encode(held_ref[index, rows] * float(2**SHIFT))

        def blend(rows, band):
            held = momentum_ref[expert_of(quarter, True, index), band].astype(jnp.float32)
            out_ref[index, rows] = encode((held_ref[index, rows] + BLEND * held) * float(2**SHIFT))

        on_band(quarter, blend)

    loop(8, expert)
    if rest:
        loop(8, lambda index: raw_copy(quarter - 1, True, parts_ref, *rest, index).wait())


def first_calls(parts, momentum):
    hbm = pl.BlockSpec(memory_space=pltpu.HBM)
    whole = pl.BlockSpec(memory_space=pltpu.VMEM)
    params = pltpu.CompilerParams(vmem_limit_bytes=40 * 1024 * 1024)

    def raw(quarter):
        return jax.ShapeDtypeStruct((8, ROWS[quarter], FF), jnp.float32)

    held = pl.pallas_call(
        fetch_kernel,
        in_specs=[hbm],
        out_specs=whole,
        scratch_shapes=[pltpu.SemaphoreType.DMA((8,))],
        out_shape=raw(3),
        compiler_params=params,
        cost_estimate=pl.CostEstimate(flops=0, bytes_accessed=64 * ROWS[3] * FF, transcendentals=0),
        name="fetch",
    )(parts)
    codes = [None] * 4
    for quarter in (3, 2, 1, 0):
        more = quarter > 0
        size = 8 * ROWS[quarter] * FF
        results = pl.pallas_call(
            functools.partial(first_kernel, quarter),
            in_specs=[hbm, whole, whole],
            out_specs=[whole] * (1 + more),
            scratch_shapes=[pltpu.SemaphoreType.DMA((8,))] * more,
            out_shape=[jax.ShapeDtypeStruct((8, ROWS[quarter], FF), jnp.bfloat16)] + [raw(quarter - 1)] * more,
            compiler_params=params,
            cost_estimate=pl.CostEstimate(flops=size * 10, bytes_accessed=size * 6, transcendentals=0),
            name=f"first_q{quarter}",
        )(parts, momentum, held)
        codes[quarter] = results[0]
        held = results[-1]
    return codes


def keep_kernel(parts_ref, momentum_ref, *refs):
    held_refs, sems = refs[4:8], refs[8]

    def copy(quarter, index):
        return raw_copy(quarter, False, parts_ref, held_refs[quarter], sems.at[quarter], index)

    for quarter in range(4):
        loop(8, lambda index, quarter=quarter: copy(quarter, index).start())
    for quarter, held_ref in enumerate(held_refs):

        def expert(index, quarter=quarter, held_ref=held_ref):
            copy(quarter, index).wait()
            for rows in strips(ROWS[quarter]):
                held_ref[index, rows] = held_ref[index, rows] * float(2**SHIFT)

            def blend(rows, band):
                held = momentum_ref[expert_of(quarter, False, index), band].astype(jnp.float32)
                held_ref[index, rows] += BLEND * float(2**SHIFT) * held

            on_band(quarter, blend)

        loop(8, expert)


def keep_call(parts, momentum, codes):
    whole = pl.BlockSpec(memory_space=pltpu.VMEM)
    return pl.pallas_call(
        keep_kernel,
        in_specs=[pl.BlockSpec(memory_space=pltpu.HBM), whole] + [pl.BlockSpec(memory_space=pl.ANY)] * 4,
        out_specs=[whole] * 4,
        scratch_shapes=[pltpu.SemaphoreType.DMA((4, 8))],
        out_shape=[jax.ShapeDtypeStruct((8, rows, FF), jnp.float32) for rows in ROWS],
        compiler_params=pltpu.CompilerParams(vmem_limit_bytes=32 * 1024 * 1024),
        cost_estimate=pl.CostEstimate(flops=8 * D * FF, bytes_accessed=64 * D * FF, transcendentals=0),
        name="keep",
    )(parts, momentum, *codes)


def fold_kernel(*refs):
    kept_refs, received, out_refs = refs[:4], refs[4:8], refs[9:]
    for kept_ref, ref, out_ref in zip(kept_refs, received, out_refs):

        def expert(index, kept_ref=kept_ref, ref=ref, out_ref=out_ref):
            for rows in strips(out_ref.shape[1]):
                out_ref[index, rows] = kept_ref[index, rows] + decode(ref[index, rows])

        loop(4, expert)


def fold_call(kept, received, after):
    whole = pl.BlockSpec(memory_space=pltpu.VMEM)
    return pl.pallas_call(
        fold_kernel,
        in_specs=[whole] * 8 + [pl.BlockSpec(memory_space=pl.ANY)],
        out_specs=[whole] * 4,
        out_shape=[jax.ShapeDtypeStruct((4, rows, FF), jnp.float32) for rows in ROWS],
        compiler_params=pltpu.CompilerParams(vmem_limit_bytes=8 * 1024 * 1024),
        cost_estimate=pl.CostEstimate(flops=32 * D * FF, bytes_accessed=40 * D * FF, transcendentals=8 * D * FF),
        name="fold",
    )(*kept, *received, after)


def step_kernel(place, base_ref, *refs):
    received, out_ref = refs[:-1], refs[-1]

    def expert(index):
        for rows in strips(out_ref.shape[1]):
            value = base_ref[place + index, rows]
            for ref in received:
                value = value + decode(ref[place + index, rows])
            out_ref[index, rows] = encode(value)

    loop(out_ref.shape[0], expert)


def step_call(quarter, step, base, received):
    count = 8 >> step
    size = count * ROWS[quarter] * FF
    whole = pl.BlockSpec(memory_space=pltpu.VMEM)
    return pl.pallas_call(
        functools.partial(step_kernel, count),
        in_specs=[whole] * (1 + len(received)),
        out_specs=whole,
        out_shape=jax.ShapeDtypeStruct((count, ROWS[quarter], FF), jnp.bfloat16),
        compiler_params=pltpu.CompilerParams(vmem_limit_bytes=8 * 1024 * 1024),
        cost_estimate=pl.CostEstimate(
            flops=size * 16, bytes_accessed=size * (6 + 2 * step), transcendentals=2 * size * step
        ),
        name=f"codes_q{quarter}_s{step}",
    )(base, *received)


def halves(value):
    high = value.astype(jnp.bfloat16)
    return high, (value - high.astype(jnp.float32)).astype(jnp.bfloat16)


def dot(left, right):
    return jnp.dot(left, right, preferred_element_type=jnp.float32)


def wide(left):
    return jnp.concatenate([left[0], left[1], left[0]], axis=1)


def tall(right):
    return jnp.concatenate([right[0], right[0], right[1]], axis=0)


def symmetric(left, right):
    left, right = wide(left), tall(right)
    most = dot(left, right[:, :SPLIT])
    corner = dot(left[SPLIT:], right[:, SPLIT:])
    return jnp.concatenate([most, jnp.concatenate([most[SPLIT:].T, corner], axis=0)], axis=1)


def split_sums(kept_ref, received, high_ref, low_ref, first):
    for rows in strips(kept_ref.shape[1]):
        value = kept_ref[0, rows]
        for ref in received:
            value = value + decode(ref[0, rows])
        out = pl.ds(first + rows.start, rows.size)
        high_ref[out], low_ref[out] = halves(value)


def gram_part(high_ref, low_ref):
    part = None
    for start in range(0, high_ref.shape[0] - BLOCK + 1, BLOCK):
        rows = pl.ds(start, BLOCK)
        high = high_ref[rows]
        more = dot(high.T, jnp.concatenate([high, low_ref[rows]], axis=1))
        part = more if part is None else part + more
    return part


def gather_kernel(*refs):
    kept_refs, received, high_ref, low_ref, part_ref = refs[:3], refs[3:12], *refs[12:]
    for place, kept_ref in enumerate(kept_refs):
        split_sums(kept_ref, received[3 * place : 3 * place + 3], high_ref, low_ref, FIRST[1 + place])
    part_ref[...] = gram_part(high_ref, low_ref)


def gather_call(kept, received):
    whole = pl.BlockSpec(memory_space=pltpu.VMEM)
    rows = FIRST[0]
    split = jax.ShapeDtypeStruct((rows, FF), jnp.bfloat16)
    return pl.pallas_call(
        gather_kernel,
        in_specs=[whole] * (len(kept) + len(received)),
        out_specs=[whole] * 3,
        out_shape=[split, split, jax.ShapeDtypeStruct((FF, 2 * FF), jnp.float32)],
        compiler_params=pltpu.CompilerParams(vmem_limit_bytes=16 * 1024 * 1024),
        cost_estimate=pl.CostEstimate(
            flops=4 * rows * FF * FF, bytes_accessed=16 * rows * FF, transcendentals=8 * rows * FF
        ),
        name="gather",
    )(*kept, *received)


def iterate_kernel(kept_ref, *refs):
    received, early_high, early_low, part_ref, out_ref, high_ref, low_ref = refs[:3], *refs[3:]
    over = FIRST[0] % BLOCK
    high_ref[pl.ds(0, over)] = early_high[pl.ds(FIRST[0] - over, over)]
    low_ref[pl.ds(0, over)] = early_low[pl.ds(FIRST[0] - over, over)]
    split_sums(kept_ref, received, high_ref, low_ref, over)
    part = part_ref[...] + gram_part(high_ref, low_ref)
    gram = part[:, :FF] + (part[:, FF:] + part[:, FF:].T)

    row = lax.broadcasted_iota(jnp.int32, (FF, FF), 0)
    column = lax.broadcasted_iota(jnp.int32, (FF, FF), 1)
    on_diagonal = row == column
    squares = jnp.sum(jnp.where(on_diagonal, gram, 0.0))
    scale = 1.0 / (jnp.sqrt(jnp.full((1, 1), squares)) + 1e-07 / GAIN * 2**SHIFT)
    a = gram * scale * scale
    power = None
    for turn in range(NS_ITERS):
        a_split = halves(a)
        b = -4.775 * a + 2.0315 * symmetric(a_split, a_split)
        b_split = halves(b)
        if turn < NS_ITERS - 1:
            once = 3.4445 * a + symmetric(a_split, b_split)
            a = 3.4445 * once + symmetric(halves(once), b_split)
        if power is None:
            power = jnp.where(on_diagonal, 3.4445, 0.0) + b
        else:
            power = 3.4445 * power + symmetric(halves(power), b_split)
    power_split = tall(halves(power * (scale * float(max(D, FF)) ** 0.5)))
    for start in range(0, D, BLOCK):
        rows = pl.ds(start, BLOCK)
        if start + BLOCK <= FIRST[0]:
            left = (early_high[rows], early_low[rows])
        else:
            left = (high_ref[...], low_ref[...])
        out_ref[rows] = dot(wide(left), power_split).astype(jnp.bfloat16)


def iterate_call(kept, received, early):
    whole = pl.BlockSpec(memory_space=pltpu.VMEM)
    return pl.pallas_call(
        iterate_kernel,
        in_specs=[whole] * (1 + len(received) + len(early)),
        out_specs=whole,
        scratch_shapes=[pltpu.VMEM((BLOCK, FF), jnp.bfloat16)] * 2,
        out_shape=jax.ShapeDtypeStruct((D, FF), jnp.bfloat16),
        compiler_params=pltpu.CompilerParams(vmem_limit_bytes=16 * 1024 * 1024),
        cost_estimate=pl.CostEstimate(
            flops=3 * 2 * FF * FF * (17 * FF + D), bytes_accessed=6 * 1024 * 1024, transcendentals=0
        ),
        name="newton_schulz",
    )(kept, *received, *early)


def local(grad_parts, momentum):
    parts = grad_parts[0]

    def send(codes, step):
        return [lax.ppermute(codes[quarter], ("rep", "exp"), partners(quarter, step)) for quarter in range(4)]

    codes = first_calls(parts, momentum)
    kept = keep_call(parts, momentum, codes)
    first = send(codes, 0)
    codes = [step_call(quarter, 1, kept[quarter], [first[quarter]]) for quarter in range(4)]
    base = fold_call(kept, first, codes[0])
    second = send(codes, 1)
    codes = [step_call(quarter, 2, base[quarter], [second[quarter]]) for quarter in range(4)]
    third = send(codes, 2)
    codes = [step_call(quarter, 3, base[quarter], [second[quarter], third[quarter]]) for quarter in range(4)]
    received = list(zip(second, third, send(codes, 3)))
    early = gather_call(base[1:], sum(received[1:], ()))
    update = iterate_call(base[0], received[0], early)
    return lax.all_to_all(update.reshape(16, BAND, FF), "rep", split_axis=0, concat_axis=0, tiled=True)


def solution(mesh):
    return jax.shard_map(
        local,
        mesh=mesh,
        in_specs=(P("rep", "exp", None, None), P("exp", "rep", None)),
        out_specs=P("exp", "rep", None),
        check_vma=False,
    )
```

```python
import functools
import math

import jax
import jax.numpy as jnp
from jax import lax
from jax.experimental import pallas as pl
from jax.experimental.pallas import tpu as pltpu
from jax.sharding import PartitionSpec as P

D = 1024
FF = 384
NS_ITERS = 5
ROWS = (240, 256, 256, 272)
FIRST = (784, 528, 272, 0)
PIECES = ((0, 16), (16, 48))
STRIP = 64
BAND = 64
SPLIT = 256
BLOCK = 256
GAIN = 1.0 + 0.95
BLEND = 0.95 * 0.95 / GAIN

ORDERS = ((3, 0, 2, 1), (1, 3, 0, 2), (2, 1, 3, 0), (0, 2, 1, 3))
FLIPS = (1, 3, 4, 12)
SHIFT = 8
POWER = 9


def flips_of(quarter, core):
    return [FLIPS[bit] for bit in ORDERS[(quarter + 3 * core) % 4]]


def partners(quarter, step):
    pairs = []
    for device in range(128):
        rep, group = divmod(device, 8)
        pairs.append((device, 8 * (rep ^ flips_of(quarter, group % 2)[step]) + group))
    return pairs


def expert_of(quarter, sent, index):
    core = lax.axis_index("exp") & 1
    first, *others = [zero + core * (one - zero) for zero, one in zip(flips_of(quarter, 0), flips_of(quarter, 1))]
    expert = lax.axis_index("rep")
    if sent:
        expert = expert ^ first
    for place, flip in enumerate(others):
        expert = expert ^ (((index >> (2 - place)) & 1) * flip)
    return expert


def encode(value):
    second = value * value
    fourth = second * second
    return (fourth * fourth * value).astype(jnp.bfloat16)


def decode(code):
    code = code.astype(jnp.float32)
    level = jnp.log(jnp.maximum(jnp.abs(code), float(2.0**-126)))
    return code * jnp.exp2(level * ((1 / POWER - 1) / math.log(2.0)))


def raw_copy(quarter, sent, parts_ref, held_ref, sems, index):
    rows = pl.ds(FIRST[quarter], ROWS[quarter])
    expert = expert_of(quarter, sent, index)
    return pltpu.make_async_copy(parts_ref.at[expert, rows], held_ref.at[index], sems.at[index])


def on_band(quarter, body):
    low, count = FIRST[quarter], ROWS[quarter]
    band_low = lax.axis_index("rep") * BAND

    @pl.when((band_low < low + count) & (band_low + BAND > low))
    def _():
        for start, size in PIECES:
            row = band_low + start - low

            @pl.when((row >= 0) & (row < count))
            def _(start=start, size=size, row=row):
                body(pl.ds(pl.multiple_of(row, 16), size), pl.ds(start, size))


def strips(count):
    return [pl.ds(start, min(STRIP, count - start)) for start in range(0, count, STRIP)]


def loop(count, body):
    def step(index, carry):
        body(index)
        return carry

    lax.fori_loop(0, count, step, 0)


def fetch_kernel(parts_ref, held_ref, sems):
    loop(8, lambda index: raw_copy(3, True, parts_ref, held_ref, sems, index).start())
    loop(8, lambda index: raw_copy(3, True, parts_ref, held_ref, sems, index).wait())


def first_kernel(quarter, parts_ref, momentum_ref, held_ref, out_ref, *rest):
    if rest:
        loop(8, lambda index: raw_copy(quarter - 1, True, parts_ref, *rest, index).start())

    def expert(index):
        for rows in strips(ROWS[quarter]):
            out_ref[index, rows] = encode(held_ref[index, rows] * float(2**SHIFT))

        def blend(rows, band):
            held = momentum_ref[expert_of(quarter, True, index), band].astype(jnp.float32)
            out_ref[index, rows] = encode((held_ref[index, rows] + BLEND * held) * float(2**SHIFT))

        on_band(quarter, blend)

    loop(8, expert)
    if rest:
        loop(8, lambda index: raw_copy(quarter - 1, True, parts_ref, *rest, index).wait())


def first_calls(parts, momentum):
    hbm = pl.BlockSpec(memory_space=pltpu.HBM)
    whole = pl.BlockSpec(memory_space=pltpu.VMEM)
    params = pltpu.CompilerParams(vmem_limit_bytes=40 * 1024 * 1024)

    def raw(quarter):
        return jax.ShapeDtypeStruct((8, ROWS[quarter], FF), jnp.float32)

    held = pl.pallas_call(
        fetch_kernel,
        in_specs=[hbm],
        out_specs=whole,
        scratch_shapes=[pltpu.SemaphoreType.DMA((8,))],
        out_shape=raw(3),
        compiler_params=params,
        cost_estimate=pl.CostEstimate(flops=0, bytes_accessed=64 * ROWS[3] * FF, transcendentals=0),
        name="fetch",
    )(parts)
    codes = [None] * 4
    for quarter in (3, 2, 1, 0):
        more = quarter > 0
        size = 8 * ROWS[quarter] * FF
        results = pl.pallas_call(
            functools.partial(first_kernel, quarter),
            in_specs=[hbm, whole, whole],
            out_specs=[whole] * (1 + more),
            scratch_shapes=[pltpu.SemaphoreType.DMA((8,))] * more,
            out_shape=[jax.ShapeDtypeStruct((8, ROWS[quarter], FF), jnp.bfloat16)] + [raw(quarter - 1)] * more,
            compiler_params=params,
            cost_estimate=pl.CostEstimate(flops=size * 10, bytes_accessed=size * 6, transcendentals=0),
            name=f"first_q{quarter}",
        )(parts, momentum, held)
        codes[quarter] = results[0]
        held = results[-1]
    return codes


def keep_kernel(parts_ref, momentum_ref, *refs):
    held_refs, sems = refs[4:8], refs[8]

    def copy(quarter, index):
        return raw_copy(quarter, False, parts_ref, held_refs[quarter], sems.at[quarter], index)

    for quarter in range(4):
        loop(8, lambda index, quarter=quarter: copy(quarter, index).start())
    for quarter, held_ref in enumerate(held_refs):

        def expert(index, quarter=quarter, held_ref=held_ref):
            copy(quarter, index).wait()
            for rows in strips(ROWS[quarter]):
                held_ref[index, rows] = held_ref[index, rows] * float(2**SHIFT)

            def blend(rows, band):
                held = momentum_ref[expert_of(quarter, False, index), band].astype(jnp.float32)
                held_ref[index, rows] += BLEND * float(2**SHIFT) * held

            on_band(quarter, blend)

        loop(8, expert)


def keep_call(parts, momentum, codes):
    whole = pl.BlockSpec(memory_space=pltpu.VMEM)
    return pl.pallas_call(
        keep_kernel,
        in_specs=[pl.BlockSpec(memory_space=pltpu.HBM), whole] + [pl.BlockSpec(memory_space=pl.ANY)] * 4,
        out_specs=[whole] * 4,
        scratch_shapes=[pltpu.SemaphoreType.DMA((4, 8))],
        out_shape=[jax.ShapeDtypeStruct((8, rows, FF), jnp.float32) for rows in ROWS],
        compiler_params=pltpu.CompilerParams(vmem_limit_bytes=32 * 1024 * 1024),
        cost_estimate=pl.CostEstimate(flops=8 * D * FF, bytes_accessed=64 * D * FF, transcendentals=0),
        name="keep",
    )(parts, momentum, *codes)


def fold_kernel(*refs):
    kept_refs, received, out_refs = refs[:4], refs[4:8], refs[9:]
    for kept_ref, ref, out_ref in zip(kept_refs, received, out_refs):

        def expert(index, kept_ref=kept_ref, ref=ref, out_ref=out_ref):
            for rows in strips(out_ref.shape[1]):
                out_ref[index, rows] = kept_ref[index, rows] + decode(ref[index, rows])

        loop(4, expert)


def fold_call(kept, received, after):
    whole = pl.BlockSpec(memory_space=pltpu.VMEM)
    return pl.pallas_call(
        fold_kernel,
        in_specs=[whole] * 8 + [pl.BlockSpec(memory_space=pl.ANY)],
        out_specs=[whole] * 4,
        out_shape=[jax.ShapeDtypeStruct((4, rows, FF), jnp.float32) for rows in ROWS],
        compiler_params=pltpu.CompilerParams(vmem_limit_bytes=8 * 1024 * 1024),
        cost_estimate=pl.CostEstimate(flops=32 * D * FF, bytes_accessed=40 * D * FF, transcendentals=8 * D * FF),
        name="fold",
    )(*kept, *received, after)


def step_kernel(place, base_ref, *refs):
    received, out_ref = refs[:-1], refs[-1]

    def expert(index):
        for rows in strips(out_ref.shape[1]):
            value = base_ref[place + index, rows]
            for ref in received:
                value = value + decode(ref[place + index, rows])
            out_ref[index, rows] = encode(value)

    loop(out_ref.shape[0], expert)


def step_call(quarter, step, base, received):
    count = 8 >> step
    size = count * ROWS[quarter] * FF
    whole = pl.BlockSpec(memory_space=pltpu.VMEM)
    return pl.pallas_call(
        functools.partial(step_kernel, count),
        in_specs=[whole] * (1 + len(received)),
        out_specs=whole,
        out_shape=jax.ShapeDtypeStruct((count, ROWS[quarter], FF), jnp.bfloat16),
        compiler_params=pltpu.CompilerParams(vmem_limit_bytes=8 * 1024 * 1024),
        cost_estimate=pl.CostEstimate(
            flops=size * 16, bytes_accessed=size * (6 + 2 * step), transcendentals=2 * size * step
        ),
        name=f"codes_q{quarter}_s{step}",
    )(base, *received)


def halves(value):
    high = value.astype(jnp.bfloat16)
    return high, (value - high.astype(jnp.float32)).astype(jnp.bfloat16)


def dot(left, right):
    return jnp.dot(left, right, preferred_element_type=jnp.float32)


def wide(left):
    return jnp.concatenate([left[0], left[1], left[0]], axis=1)


def tall(right):
    return jnp.concatenate([right[0], right[0], right[1]], axis=0)


def symmetric(left, right):
    left, right = wide(left), tall(right)
    most = dot(left, right[:, :SPLIT])
    corner = dot(left[SPLIT:], right[:, SPLIT:])
    return jnp.concatenate([most, jnp.concatenate([most[SPLIT:].T, corner], axis=0)], axis=1)


def split_sums(kept_ref, received, high_ref, low_ref, first):
    for rows in strips(kept_ref.shape[1]):
        value = kept_ref[0, rows]
        for ref in received:
            value = value + decode(ref[0, rows])
        out = pl.ds(first + rows.start, rows.size)
        high_ref[out], low_ref[out] = halves(value)


def gram_part(high_ref, low_ref):
    part = None
    for start in range(0, high_ref.shape[0] - BLOCK + 1, BLOCK):
        rows = pl.ds(start, BLOCK)
        high = high_ref[rows]
        more = dot(high.T, jnp.concatenate([high, low_ref[rows]], axis=1))
        part = more if part is None else part + more
    return part[:, :FF] + (part[:, FF:] + part[:, FF:].T)


def gather_kernel(*refs):
    kept_refs, received, high_ref, low_ref, part_ref = refs[:3], refs[3:12], *refs[12:]
    for place, kept_ref in enumerate(kept_refs):
        split_sums(kept_ref, received[3 * place : 3 * place + 3], high_ref, low_ref, FIRST[1 + place])
    part_ref[...] = gram_part(high_ref, low_ref)


def gather_call(kept, received):
    whole = pl.BlockSpec(memory_space=pltpu.VMEM)
    rows = FIRST[0]
    split = jax.ShapeDtypeStruct((rows, FF), jnp.bfloat16)
    return pl.pallas_call(
        gather_kernel,
        in_specs=[whole] * (len(kept) + len(received)),
        out_specs=[whole] * 3,
        out_shape=[split, split, jax.ShapeDtypeStruct((FF, FF), jnp.float32)],
        compiler_params=pltpu.CompilerParams(vmem_limit_bytes=16 * 1024 * 1024),
        cost_estimate=pl.CostEstimate(
            flops=4 * rows * FF * FF, bytes_accessed=16 * rows * FF, transcendentals=8 * rows * FF
        ),
        name="gather",
    )(*kept, *received)


def iterate_kernel(kept_ref, *refs):
    received, early_high, early_low, part_ref, out_ref, high_ref, low_ref = refs[:3], *refs[3:]
    over = FIRST[0] % BLOCK
    high_ref[pl.ds(0, over)] = early_high[pl.ds(FIRST[0] - over, over)]
    low_ref[pl.ds(0, over)] = early_low[pl.ds(FIRST[0] - over, over)]
    split_sums(kept_ref, received, high_ref, low_ref, over)
    gram = part_ref[...] + gram_part(high_ref, low_ref)

    row = lax.broadcasted_iota(jnp.int32, (FF, FF), 0)
    column = lax.broadcasted_iota(jnp.int32, (FF, FF), 1)
    on_diagonal = row == column
    squares = jnp.sum(jnp.where(on_diagonal, gram, 0.0))
    scale = 1.0 / (jnp.sqrt(jnp.full((1, 1), squares)) + 1e-07 / GAIN * 2**SHIFT)
    a = gram * scale * scale
    power = None
    for turn in range(NS_ITERS):
        a_split = halves(a)
        b = -4.775 * a + 2.0315 * symmetric(a_split, a_split)
        b_split = halves(b)
        if turn < NS_ITERS - 1:
            once = 3.4445 * a + symmetric(a_split, b_split)
            a = 3.4445 * once + symmetric(halves(once), b_split)
        if power is None:
            power = jnp.where(on_diagonal, 3.4445, 0.0) + b
        else:
            power = 3.4445 * power + symmetric(halves(power), b_split)
    power_split = tall(halves(power * (scale * float(max(D, FF)) ** 0.5)))
    for start in range(0, D, BLOCK):
        rows = pl.ds(start, BLOCK)
        if start + BLOCK <= FIRST[0]:
            left = (early_high[rows], early_low[rows])
        else:
            left = (high_ref[...], low_ref[...])
        out_ref[rows] = dot(wide(left), power_split).astype(jnp.bfloat16)


def iterate_call(kept, received, early):
    whole = pl.BlockSpec(memory_space=pltpu.VMEM)
    return pl.pallas_call(
        iterate_kernel,
        in_specs=[whole] * (1 + len(received) + len(early)),
        out_specs=whole,
        scratch_shapes=[pltpu.VMEM((BLOCK, FF), jnp.bfloat16)] * 2,
        out_shape=jax.ShapeDtypeStruct((D, FF), jnp.bfloat16),
        compiler_params=pltpu.CompilerParams(vmem_limit_bytes=16 * 1024 * 1024),
        cost_estimate=pl.CostEstimate(
            flops=3 * 2 * FF * FF * (17 * FF + D), bytes_accessed=6 * 1024 * 1024, transcendentals=0
        ),
        name="newton_schulz",
    )(kept, *received, *early)


def local(grad_parts, momentum):
    parts = grad_parts[0]

    def send(codes, step):
        return [lax.ppermute(codes[quarter], ("rep", "exp"), partners(quarter, step)) for quarter in range(4)]

    codes = first_calls(parts, momentum)
    kept = keep_call(parts, momentum, codes)
    first = send(codes, 0)
    codes = [step_call(quarter, 1, kept[quarter], [first[quarter]]) for quarter in range(4)]
    base = fold_call(kept, first, codes[0])
    second = send(codes, 1)
    codes = [step_call(quarter, 2, base[quarter], [second[quarter]]) for quarter in range(4)]
    third = send(codes, 2)
    codes = [step_call(quarter, 3, base[quarter], [second[quarter], third[quarter]]) for quarter in range(4)]
    received = list(zip(second, third, send(codes, 3)))
    early = gather_call(base[1:], sum(received[1:], ()))
    update = iterate_call(base[0], received[0], early)
    return lax.all_to_all(update.reshape(16, BAND, FF), "rep", split_axis=0, concat_axis=0, tiled=True)


def solution(mesh):
    return jax.shard_map(
        local,
        mesh=mesh,
        in_specs=(P("rep", "exp", None, None), P("exp", "rep", None)),
        out_specs=P("exp", "rep", None),
        check_vma=False,
    )
```
